768 devices in a mesh: tensor: 8 (over x, y_hi), dp: 96 (over y_lo, z, core).
Axes of the slice: x: 4, y: 8 (y_hi: 2, y_lo: 4; y = y_hi * 4 + y_lo), z: 12, core: 2. Of those that a mesh axis runs over, the one named last changes fastest.
Arguments:
- gate: bfloat16 [192, 36864], P('dp', 'tensor'), may hold values from -6 to 6
- up: bfloat16 [192, 36864], P('dp', 'tensor'), may hold values from -6 to 6
- down_weight: bfloat16 [36864, 18432], P('tensor', 'dp'), may hold values from -0.03125 to 0.03125
- out_grad: bfloat16 [192, 18432], P('tensor', 'dp'), may hold values from -20 to 20
Outputs:
- output: bfloat16 [192, 18432], P('tensor', 'dp')
- grad_down: bfloat16 [36864, 18432], P('tensor', 'dp')
- grad_gate: bfloat16 [192, 36864], P('dp', 'tensor')
- grad_up: bfloat16 [192, 36864], P('dp', 'tensor')
The draws below stay inside these ranges and needn't reach their ends.
All inputs are finite; a program needn't handle non-finite values.
Results may differ from the reference program's by a relative error of at most 0.0049.
Values may be sent and summed in bfloat16 or wider, within the bound.
No kernel may reach another device: no remote copies, remote signals or barrier semaphores. Data moves between devices by JAX's collectives and lax.ppermute only.
A program may use at most 32 MiB of HBM per device.

```python
import jax
import jax.numpy as jnp

D = 18432
FF = 36864
TOKENS = 192


def raised(drawn, key, source, target, shards_of, factor):
    owner, partner = [(jnp.arange(drawn.shape[position]) // (drawn.shape[position] // shards_of)).reshape([-1 if axis == position else 1 for axis in range(drawn.ndim)]) for position in (source, target)]
    chosen = jax.random.permutation(key, shards_of)[partner]
    strong = (owner == chosen) | (owner == (partner + shards_of // 2) % shards_of)
    return jnp.where(strong, factor * drawn, drawn)


def block_levels(key, shape, cuts, smallest, largest):
    gain, own = 1.0, jax.random.fold_in(key, 6)
    for axis_at, shards_of in cuts:
        heights = jnp.exp(jax.random.uniform(jax.random.fold_in(own, axis_at), (shards_of,), jnp.float32, smallest / len(cuts), largest / len(cuts)))
        gain = gain * jnp.repeat(heights, shape[axis_at] // shards_of).reshape([-1 if axis == axis_at else 1 for axis in range(len(shape))])
    return gain


def noise(key, dims, spread, bound, pieces=(), dtype=jnp.bfloat16):
    gain = block_levels(key, dims, pieces, -0.22, 0.18) if pieces else 1.0
    entries = jax.random.normal(key, dims, jnp.float32) * spread * gain
    return jnp.minimum(jnp.maximum(entries, -bound), bound).astype(dtype)


def heavy_noise(stream_key, shape, deviation, most, shards, heavy, held_as=jnp.bfloat16):
    drawn = deviation * jax.random.normal(stream_key, shape, jnp.float32)
    if shards:
        drawn = drawn * block_levels(stream_key, shape, shards, -0.22, 0.18)
    return jnp.clip(raised(drawn, jax.random.fold_in(stream_key, 3), *heavy), -most, most).astype(held_as)


def setup_inputs(seed: int = 0) -> dict:
    streams_of = jax.random.split(jax.random.key(seed), 5)
    return {
        "gate": noise(streams_of[0], (TOKENS, FF), 1.0, 6.0, ((0, 96), (1, 8))),
        "up": noise(streams_of[1], (TOKENS, FF), 1.0, 6.0, ((0, 96), (1, 8))),
        "down_weight": noise(streams_of[2], (FF, D), FF ** -0.5, 0.03125, ((0, 8), (1, 96))),
        "out_grad": heavy_noise(streams_of[3], (TOKENS, D), 1.0, 20.0, ((0, 8), (1, 96)), (1, 0, 96, 4.75)),
    }


def reference(gate, up, down_weight, out_grad):
    gate32 = gate.astype(jnp.float32)
    up32 = up.astype(jnp.float32)
    sigmoid = jax.nn.sigmoid(gate32)
    silu = gate32 * sigmoid
    hidden = (silu * up32).astype(jnp.bfloat16)
    output = jnp.dot(hidden, down_weight, preferred_element_type=jnp.float32).astype(jnp.bfloat16)
    grad_down = jnp.dot(hidden.T, out_grad, preferred_element_type=jnp.float32).astype(jnp.bfloat16)
    hidden_grad = jnp.dot(out_grad, down_weight.T, preferred_element_type=jnp.float32)
    grad_gate = (hidden_grad * up32 * sigmoid * (1.0 + gate32 * (1.0 - sigmoid))).astype(jnp.bfloat16)
    grad_up = (hidden_grad * silu).astype(jnp.bfloat16)
    return output, grad_down, grad_gate, grad_up
```

```python
import numpy as np

import jax
import jax.numpy as jnp
from jax import lax
from jax.sharding import PartitionSpec as P

YL, Z, C = 4, 12, 2
NEAR = 4
FAR = Z // NEAR


def dp_index(yl, z, c):
    return (yl * Z + z) * C + c


WIDE = [[dp_index(y, z, 0) for z in range(Z)] for y in range(YL)] + [
    [dp_index(y, n + NEAR * f, 1) for y in range(YL) for f in range(FAR)] for n in range(NEAR)
]
NARROW = [[dp_index(y, z, 0) for y in range(YL)] for z in range(Z)] + [
    [dp_index(y, n + NEAR * f, 1) for n in range(NEAR)] for y in range(YL) for f in range(FAR)
]
ORDER = [dp_index(y, z, 0) for y in range(YL) for z in range(Z)] + [
    dp_index(y, n + NEAR * f, 1) for n in range(NEAR) for y in range(YL) for f in range(FAR)
]
SWAP = [(i, i ^ 1) for i in range(YL * Z * C)]
f32, bf16 = jnp.float32, jnp.bfloat16


def row_order(each):
    return np.array([[i * each + r for r in range(each)] for i in ORDER], np.int32).reshape(-1)


def exchange(blocks, groups):
    return lax.all_to_all(blocks, "dp", 0, 0, axis_index_groups=groups)


def total(blocks):
    parts = [blocks[i].astype(f32) for i in range(blocks.shape[0])]
    while len(parts) > 1:
        parts = [a + b for a, b in zip(parts[::2], parts[1::2])] + parts[len(parts) // 2 * 2 :]
    return parts[0]


def dot(a, b, ca, cb):
    return lax.dot_general(a, b, (((ca,), (cb,)), ((), ())), preferred_element_type=f32)


def tie(*arrays):
    return lax.optimization_barrier(arrays)

BACK = [group[::-1] for group in WIDE]


def partner(mask, members):
    return [(i, i ^ mask) for i in range(members)]


def gather_tokens(rows):
    for mask in (1, 2, 4):
        rows = jnp.concatenate([rows, lax.ppermute(rows, "tensor", partner(mask, 8))], axis=0)
    return rows


def scatter_tokens(rows):
    for mask in (4, 2, 1):
        half = rows.shape[0] // 2
        theirs = lax.ppermute(rows[half:].astype(bf16), "tensor", partner(mask, 8))
        rows = rows[:half].astype(f32) + theirs.astype(f32)
    return rows


def placement(each, tokens):
    core = lax.axis_index("dp") % C
    mine = lax.axis_index("tensor")
    rows = row_order(each)
    token_at = jnp.where(core == 0, rows, np.roll(rows, tokens // 2))
    column = jnp.arange(tokens, dtype=jnp.int32)
    own = tokens // 8
    token_of = jnp.bitwise_xor(mine, column // own) * own + column % own
    return (token_at[:, None] == token_of[None, :]).astype(bf16)


def local(gate, up, down_weight, out_grad):
    each, units = gate.shape
    own, width = out_grad.shape
    tokens = own * 8
    half = tokens // 2
    few = half // 4
    place = placement(each, tokens)

    gate32 = gate.astype(f32)
    up32 = up.astype(f32)
    sigmoid = jax.nn.sigmoid(gate32)
    silu = gate32 * sigmoid
    hidden = (silu * up32).astype(bf16)

    h1 = exchange(jnp.broadcast_to(hidden[None], (12, each, units)), WIDE).reshape(few, units)

    grads = dot(place, gather_tokens(out_grad), 1, 0).astype(bf16)
    received = lax.ppermute(dot(grads[half:], down_weight, 1, 1).astype(bf16), "dp", SWAP)
    r1 = (dot(grads[:half], down_weight, 1, 1) + received.astype(f32)).astype(bf16)

    h2 = exchange(jnp.broadcast_to(h1[None], (4, few, units)), NARROW).reshape(half, units)
    h2, r1 = tie(h2, r1)
    r2 = total(exchange(r1.reshape(4, few, units), NARROW)).astype(bf16).reshape(12, each, units)
    r3 = exchange(r2[::-1], BACK)
    other = lax.ppermute(h2, "dp", SWAP)
    partial_out = jnp.concatenate(
        [dot(h2, down_weight, 1, 0).astype(bf16), dot(other, down_weight, 1, 0).astype(bf16)], axis=0
    )
    output = scatter_tokens(dot(place, partial_out, 0, 0)).astype(bf16)

    hidden_grad = total(r3)
    grad_down = dot(jnp.concatenate([h2, other], axis=0), grads, 0, 0).astype(bf16)
    grad_gate = (hidden_grad * up32 * sigmoid * (1.0 + gate32 * (1.0 - sigmoid))).astype(bf16)
    grad_up = (hidden_grad * silu).astype(bf16)
    return (output, grad_down, grad_gate, grad_up)


def solution(mesh):
    placed = (P("dp", "tensor"), P("dp", "tensor"), P("tensor", "dp"), P("tensor", "dp"))
    return jax.shard_map(
        local,
        mesh=mesh,
        in_specs=placed,
        out_specs=(P("tensor", "dp"), P("tensor", "dp"), P("dp", "tensor"), P("dp", "tensor")),
        check_vma=False,
    )
```

```python
import numpy as np

import jax
import jax.numpy as jnp
from jax import lax
from jax.sharding import PartitionSpec as P

YL, Z, C = 4, 12, 2
NEAR = 4
FAR = Z // NEAR


def dp_index(yl, z, c):
    return (yl * Z + z) * C + c


WIDE = [[dp_index(y, z, 0) for z in range(Z)] for y in range(YL)] + [
    [dp_index(y, n + NEAR * f, 1) for y in range(YL) for f in range(FAR)] for n in range(NEAR)
]
BACK = [group[::-1] for group in WIDE]
NARROW = [[dp_index(y, z, 0) for y in range(YL)] for z in range(Z)] + [
    [dp_index(y, n + NEAR * f, 1) for n in range(NEAR)] for y in range(YL) for f in range(FAR)
]
SWAP = [(i, i ^ 1) for i in range(YL * Z * C)]
f32, bf16 = jnp.float32, jnp.bfloat16


def row_order(each, back):
    order = [i for group in (BACK if back else WIDE) for i in group]
    return np.array([[i * each + r for r in range(each)] for i in order], np.int32).reshape(-1)


def exchange(blocks, groups):
    return lax.all_to_all(blocks, "dp", 0, 0, axis_index_groups=groups)


def total(blocks):
    parts = [blocks[i].astype(f32) for i in range(blocks.shape[0])]
    while len(parts) > 1:
        parts = [a + b for a, b in zip(parts[::2], parts[1::2])] + parts[len(parts) // 2 * 2 :]
    return parts[0]


def dot(a, b, ca, cb):
    return lax.dot_general(a, b, (((ca,), (cb,)), ((), ())), preferred_element_type=f32)


def tie(*arrays):
    return lax.optimization_barrier(arrays)


def partner(mask, members):
    return [(i, i ^ mask) for i in range(members)]


def gather_tokens(rows):
    for mask in (1, 2, 4):
        rows = jnp.concatenate([rows, lax.ppermute(rows, "tensor", partner(mask, 8))], axis=0)
    return rows


def scatter_tokens(rows):
    for mask in (4, 2, 1):
        half = rows.shape[0] // 2
        theirs = lax.ppermute(rows[half:].astype(bf16), "tensor", partner(mask, 8))
        rows = rows[:half].astype(f32) + theirs.astype(f32)
    return rows


def placement(each, tokens, back):
    core = lax.axis_index("dp") % C
    mine = lax.axis_index("tensor")
    rows = row_order(each, back)
    token_at = jnp.where(core == 0, rows, np.roll(rows, tokens // 2))
    column = jnp.arange(tokens, dtype=jnp.int32)
    own = tokens // 8
    token_of = jnp.bitwise_xor(mine, column // own) * own + column % own
    return (token_at[:, None] == token_of[None, :]).astype(bf16)


def local(gate, up, down_weight, out_grad):
    each, units = gate.shape
    own, width = out_grad.shape
    tokens = own * 8
    half = tokens // 2
    few = half // 4
    place = placement(each, tokens, False)
    place_back = placement(each, tokens, True)

    gate_in, up_in = (a.astype(f32) for a in tie(gate, up))
    hidden = (gate_in * jax.nn.sigmoid(gate_in) * up_in).astype(bf16)
    copies = jnp.broadcast_to(hidden[None], (12, each, units))

    h1 = exchange(copies, WIDE).reshape(few, units)

    rows = gather_tokens(out_grad)
    grads = dot(place_back, rows, 1, 0).astype(bf16)
    received = lax.ppermute(dot(grads[half:], down_weight, 1, 1).astype(bf16), "dp", SWAP)
    r1 = (dot(grads[:half], down_weight, 1, 1) + received.astype(f32)).astype(bf16)

    h2 = exchange(jnp.broadcast_to(h1[None], (4, few, units)), NARROW).reshape(half, units)
    h2, r1 = tie(h2, r1)
    r2 = total(exchange(r1.reshape(4, few, units), NARROW)).astype(bf16).reshape(12, each, units)
    r3 = exchange(r2, BACK)
    other = lax.ppermute(h2, "dp", SWAP)
    partial_out = jnp.concatenate(
        [dot(h2, down_weight, 1, 0).astype(bf16), dot(other, down_weight, 1, 0).astype(bf16)], axis=0
    )
    output = scatter_tokens(dot(place, partial_out, 0, 0)).astype(bf16)

    gate32 = gate.astype(f32)
    up32 = up.astype(f32)
    sigmoid = jax.nn.sigmoid(gate32)
    silu = gate32 * sigmoid
    hidden_grad = total(r3)
    grads = dot(place, rows, 1, 0).astype(bf16)
    grad_down = dot(jnp.concatenate([h2, other], axis=0), grads, 0, 0).astype(bf16)
    grad_gate = (hidden_grad * up32 * sigmoid * (1.0 + gate32 * (1.0 - sigmoid))).astype(bf16)
    grad_up = (hidden_grad * silu).astype(bf16)
    return (output, grad_down, grad_gate, grad_up)


def solution(mesh):
    placed = (P("dp", "tensor"), P("dp", "tensor"), P("tensor", "dp"), P("tensor", "dp"))
    return jax.shard_map(
        local,
        mesh=mesh,
        in_specs=placed,
        out_specs=(P("tensor", "dp"), P("tensor", "dp"), P("dp", "tensor"), P("dp", "tensor")),
        check_vma=False,
    )
```

```python
import numpy as np

import jax
import jax.numpy as jnp
from jax import lax
from jax.experimental import pallas as pl
from jax.experimental.pallas import tpu as pltpu
from jax.sharding import PartitionSpec as P

YL, Z, C = 4, 12, 2
NEAR = 4
FAR = Z // NEAR


def dp_index(yl, z, c):
    return (yl * Z + z) * C + c


WIDE = [[dp_index(y, z, 0) for z in range(Z)] for y in range(YL)] + [
    [dp_index(y, n + NEAR * f, 1) for y in range(YL) for f in range(FAR)] for n in range(NEAR)
]
BACK = [group[::-1] for group in WIDE]
NARROW = [[dp_index(y, z, 0) for y in range(YL)] for z in range(Z)] + [
    [dp_index(y, n + NEAR * f, 1) for n in range(NEAR)] for y in range(YL) for f in range(FAR)
]
SWAP = [(i, i ^ 1) for i in range(YL * Z * C)]
f32, bf16 = jnp.float32, jnp.bfloat16


def row_order(each, back):
    order = [i for group in (BACK if back else WIDE) for i in group]
    return np.array([[i * each + r for r in range(each)] for i in order], np.int32).reshape(-1)


def exchange(blocks, groups):
    return lax.all_to_all(blocks, "dp", 0, 0, axis_index_groups=groups)


def total(blocks):
    parts = [blocks[i].astype(f32) for i in range(blocks.shape[0])]
    while len(parts) > 1:
        parts = [a + b for a, b in zip(parts[::2], parts[1::2])] + parts[len(parts) // 2 * 2 :]
    return parts[0]


def dot(a, b, ca, cb):
    return lax.dot_general(a, b, (((ca,), (cb,)), ((), ())), preferred_element_type=f32)


def fold_kernel(blocks_ref, out_ref):
    sums = total(blocks_ref)
    each = out_ref.shape[1]
    for j in range(out_ref.shape[0]):
        out_ref[j] = sums[j * each : (j + 1) * each].astype(bf16)


def fold(blocks, each):
    count, few, units = blocks.shape
    return pl.pallas_call(
        fold_kernel,
        in_specs=[pl.BlockSpec(memory_space=pltpu.VMEM)],
        out_specs=pl.BlockSpec(memory_space=pltpu.VMEM),
        out_shape=jax.ShapeDtypeStruct((few // each, each, units), bf16),
        compiler_params=pltpu.CompilerParams(vmem_limit_bytes=8 * 2**20),
        cost_estimate=pl.CostEstimate(
            flops=blocks.size, bytes_accessed=2 * blocks.size + 2 * few * units, transcendentals=0
        ),
    )(blocks)


def tie(*arrays):
    return lax.optimization_barrier(arrays)


def partner(mask, members):
    return [(i, i ^ mask) for i in range(members)]


def gather_tokens(rows):
    for mask in (1, 2, 4):
        rows = jnp.concatenate([rows, lax.ppermute(rows, "tensor", partner(mask, 8))], axis=0)
    return rows


def scatter_tokens(rows):
    for mask in (4, 2, 1):
        half = rows.shape[0] // 2
        theirs = lax.ppermute(rows[half:].astype(bf16), "tensor", partner(mask, 8))
        rows = rows[:half].astype(f32) + theirs.astype(f32)
    return rows


def placement(each, tokens, back):
    core = lax.axis_index("dp") % C
    mine = lax.axis_index("tensor")
    rows = row_order(each, back)
    token_at = jnp.where(core == 0, rows, np.roll(rows, tokens // 2))
    column = jnp.arange(tokens, dtype=jnp.int32)
    own = tokens // 8
    token_of = jnp.bitwise_xor(mine, column // own) * own + column % own
    return (token_at[:, None] == token_of[None, :]).astype(bf16)


def local(gate, up, down_weight, out_grad):
    each, units = gate.shape
    own, width = out_grad.shape
    tokens = own * 8
    half = tokens // 2
    few = half // 4
    place = placement(each, tokens, False)
    place_back = placement(each, tokens, True)

    gate_in, up_in = (a.astype(f32) for a in tie(gate, up))
    hidden = (gate_in * jax.nn.sigmoid(gate_in) * up_in).astype(bf16)
    copies = jnp.broadcast_to(hidden[None], (12, each, units))

    h1 = exchange(copies, WIDE).reshape(few, units)

    rows = gather_tokens(out_grad)
    grads = dot(place_back, rows, 1, 0).astype(bf16)
    received = lax.ppermute(dot(grads[half:], down_weight, 1, 1).astype(bf16), "dp", SWAP)
    r1 = (dot(grads[:half], down_weight, 1, 1) + received.astype(f32)).astype(bf16)

    h2 = exchange(jnp.broadcast_to(h1[None], (4, few, units)), NARROW).reshape(half, units)
    h2, r1 = tie(h2, r1)
    r2 = fold(exchange(r1.reshape(4, few, units), NARROW), each)
    r3 = exchange(r2, BACK)
    other = lax.ppermute(h2, "dp", SWAP)
    partial_out = jnp.concatenate(
        [dot(h2, down_weight, 1, 0).astype(bf16), dot(other, down_weight, 1, 0).astype(bf16)], axis=0
    )
    output = scatter_tokens(dot(place, partial_out, 0, 0)).astype(bf16)

    gate32 = gate.astype(f32)
    up32 = up.astype(f32)
    sigmoid = jax.nn.sigmoid(gate32)
    silu = gate32 * sigmoid
    hidden_grad = total(r3)
    grads = dot(place, rows, 1, 0).astype(bf16)
    grad_down = dot(jnp.concatenate([h2, other], axis=0), grads, 0, 0).astype(bf16)
    grad_gate = (hidden_grad * up32 * sigmoid * (1.0 + gate32 * (1.0 - sigmoid))).astype(bf16)
    grad_up = (hidden_grad * silu).astype(bf16)
    return (output, grad_down, grad_gate, grad_up)


def solution(mesh):
    placed = (P("dp", "tensor"), P("dp", "tensor"), P("tensor", "dp"), P("tensor", "dp"))
    return jax.shard_map(
        local,
        mesh=mesh,
        in_specs=placed,
        out_specs=(P("tensor", "dp"), P("tensor", "dp"), P("dp", "tensor"), P("dp", "tensor")),
        check_vma=False,
    )
```
